32 devices in a mesh: section: 4 (over x, core), ep: 8 (over z, y).
Axes of the slice: x: 2, y: 2, z: 4, core: 2. Of those that a mesh axis runs over, the one named last changes fastest.
Arguments:
- states: bfloat16 [4, 1024, 6144], P('section', 'ep'), may hold values from -6 to 6
- expert_ids: int32 [4, 1024, 2], P('section', 'ep'), may hold values from 0 to 7, all different within a row; in each aligned block of 128 rows (0 to 127, 128 to 255, ..., all dimensions but the last counted through in order) at most 48 rows name the same one
- gate_values: float32 [4, 1024, 2], P('section', 'ep'), may hold values from 0.1 to 1
- keep_mask: int32 [4, 1024, 2], P('section', 'ep'), may hold values 0 or 1
- w_gate: bfloat16 [4, 6144, 16384], P('section', None, 'ep'), may hold values from -0.078125 to 0.078125
- w_up: bfloat16 [4, 6144, 16384], P('section', None, 'ep'), may hold values from -0.078125 to 0.078125
- w_down: bfloat16 [4, 16384, 6144], P('section', 'ep'), may hold values from -0.0625 to 0.0625
Outputs:
- next_states: bfloat16 [4, 1024, 6144], P('section', 'ep')
The draws below stay inside these ranges and needn't reach their ends.
Inputs may be any that keep to these rules, and one draw needn't show every extreme that they name: `expert_ids`: in every section and every aligned block of 128 tokens (the rows of one index of ep), no expert is named by more than 48 tokens, a bound that some block reaches; the 2 experts of a token differ.
All inputs are finite; a program needn't handle non-finite values. No bound on the sum of `keep_mask` on one device may be relied on, other than what follows from the above.
Results may differ from the reference program's by a relative error of at most 0.0057.
Values may be sent and summed in bfloat16 or wider, within the bound.
A program may use at most 128 MiB of HBM per device.

```python
import math
import jax
import jax.numpy as jnp
import numpy as np
from jax import lax

D = 6144
EXPERTS = 8
TOPK = 2
FF = 8192
EXP_WIN = 2
TOK_DEV = 128
CAP = 48
SECTIONS = 4
SLICES = 4
FFD = 2048
TOKENS = 1024
N_EP = 8


def plant(values, stream_key, least, largest):
    shape = values.shape
    place = [jax.random.randint(jax.random.fold_in(stream_key, axis), (), 0, shape[axis]) for axis in range(len(shape))]
    values = values.at[tuple(place)].set(least)
    longest = shape.index(max(shape))
    place[longest] = (place[longest] + 1) % shape[longest]
    return values.at[tuple(place)].set(largest)


def block_scale(stream_key, shape, pieces, least, top_value):
    level, own = 1.0, jax.random.fold_in(stream_key, 6)
    for axis_at, blocks in pieces:
        steps = jnp.exp(jax.random.uniform(jax.random.fold_in(own, axis_at), (blocks,), jnp.float32, least / len(pieces), top_value / len(pieces)))
        level = level * jnp.repeat(steps, shape[axis_at] // blocks).reshape([-1 if axis == axis_at else 1 for axis in range(len(shape))])
    return level


def deal_out(key, own, number, rows, count, top, reach, lean):
    order = jax.random.permutation(key, count)
    packed, usual = load_shares(count, rows * top, reach, lean, True), load_shares(count, rows * top, reach, lean, False)
    places = jnp.arange(count)

    def named(lengths, offset_by):
        used = int((lengths > 0).sum())
        fixed = max(1, used // 4)
        passed = fixed + (places - fixed + offset_by * (used - fixed)) % max(1, count - fixed)
        return jnp.zeros((count,), jnp.int32).at[order[jnp.where(places < fixed, places, passed)]].set(jnp.asarray(lengths, jnp.int32))

    lengths = jnp.where(number % 4 == 0, named(packed, number // 4), named(usual, number - number // 4 - 1))
    mixed = jax.random.permutation(jax.random.fold_in(own, 3), count)
    source_of, sink = mixed[0:count // 2 * 2:2], mixed[1:count // 2 * 2:2]
    margin = jnp.minimum(lengths[source_of] - 1, reach - lengths[sink]) // 2
    margin = jnp.where((source_of == order[0]) | (sink == order[0]) | (lengths[sink] == 0), 0, jnp.maximum(margin, 0))
    passed = jax.random.randint(jax.random.fold_in(own, 4), (count // 2,), 0, 1 << 20) % (margin + 1)
    lengths = lengths.at[source_of].add(-passed).at[sink].add(passed)
    members = jnp.searchsorted(jnp.cumsum(lengths), jnp.arange(rows * top), side="right").astype(jnp.int32)
    table = members.reshape(top, rows).T
    table = table[jax.random.permutation(jax.random.fold_in(own, 1), rows)]
    offset_by = jax.random.randint(jax.random.fold_in(own, 2), (rows, 1), 0, top)
    return jnp.take_along_axis(table, (jnp.arange(top)[None, :] + offset_by) % top, axis=1)


def load_shares(count, total, reach, lean, full):
    weights = [(1 << 20) // math.isqrt(rank ** lean) + 1 for rank in range(1, count + 1)]
    largest = reach if full else min(reach, max(-(-total // count), total * weights[0] // sum(weights)))
    least = 1 if total - largest >= count - 1 else 0
    counts, spare = [largest] + [least] * (count - 1), total - largest - least * (count - 1)
    while spare > 0:
        candidates = [i for i in range(1, count) if counts[i] < largest] or [i for i in range(1, count) if counts[i] < reach]
        whole, budget = sum([weights[i] for i in candidates]), spare
        for i in candidates:
            extra = min(reach - counts[i], max(1, budget * weights[i] // whole), spare)
            counts[i] = counts[i] + extra
            spare = spare - extra
    return np.array(counts)


def scatter_about(stream_key, shape, spread, limit, split=(), kind=jnp.bfloat16):
    entries = spread * jax.random.normal(stream_key, shape, jnp.float32)
    if split:
        entries = entries * block_scale(stream_key, shape, split, -0.22, 0.18)
    return jnp.clip(entries, -limit, limit).astype(kind)


def setup_inputs(seed: int = 0) -> dict:
    streams_of = jax.random.split(jax.random.key(seed), 8)
    states = scatter_about(streams_of[0], (SECTIONS, TOKENS, D), 1.0, 6.0, ((0, 4), (1, 8)))
    expert_ids_keys = jax.random.split(jax.random.fold_in(streams_of[1], 1), SECTIONS * TOKENS // TOK_DEV)
    expert_ids_turns = jax.random.permutation(jax.random.fold_in(streams_of[1], 3), SECTIONS * TOKENS // TOK_DEV)
    expert_ids = jax.vmap(lambda own, number: deal_out(jax.random.fold_in(streams_of[1], 2), own, number, TOK_DEV, EXPERTS, TOPK, CAP, 2))(expert_ids_keys, expert_ids_turns).reshape((SECTIONS, TOKENS, TOPK))
    gate_values = jnp.clip(0.1 + 0.9 * jax.random.uniform(streams_of[2], (SECTIONS, TOKENS, TOPK), jnp.float32) ** block_scale(streams_of[2], (SECTIONS, TOKENS, TOPK), ((0, 4), (1, 8)), -0.2, 0.2), 0.1, 1.0)
    keep_mask = plant((jax.random.randint(streams_of[3], (SECTIONS, TOKENS, TOPK), 0, 8) < 7).astype(jnp.int32), jax.random.fold_in(streams_of[3], 1), 0, 1)
    w_gate = scatter_about(streams_of[4], (SECTIONS, D, EXP_WIN * FF), D ** -0.5, 0.078125, ((0, 4), (2, 8)))
    w_up = scatter_about(streams_of[5], (SECTIONS, D, EXP_WIN * FF), D ** -0.5, 0.078125, ((0, 4), (2, 8)))
    w_down = scatter_about(streams_of[6], (SECTIONS, EXP_WIN * FF, D), FF ** -0.5, 0.0625, ((0, 4), (1, 8)))
    return {"states": states, "expert_ids": expert_ids, "gate_values": gate_values, "keep_mask": keep_mask, "w_gate": w_gate, "w_up": w_up, "w_down": w_down}


def expert_apply(rows_sel, gate_e, up_e, down_e):
    gate_proj = jnp.dot(rows_sel, gate_e, preferred_element_type=jnp.float32)
    up_proj = jnp.dot(rows_sel, up_e, preferred_element_type=jnp.float32)
    hidden = (jax.nn.silu(gate_proj) * up_proj).astype(jnp.bfloat16)

    def add_slice(total, index):
        part_hidden = lax.dynamic_slice_in_dim(hidden, (index * FFD).astype(jnp.int32), FFD, 1)
        part_weight = lax.dynamic_slice_in_dim(down_e, (index * FFD).astype(jnp.int32), FFD, 0)
        term = jnp.dot(part_hidden, part_weight, preferred_element_type=jnp.float32).astype(jnp.bfloat16)
        term = lax.optimization_barrier(term)
        return total + term.astype(jnp.float32), None

    start_total = jnp.zeros((rows_sel.shape[0], down_e.shape[1]), jnp.float32)
    total, unused = lax.scan(add_slice, start_total, jnp.arange(SLICES, dtype=jnp.int32))
    return total


def reference(states, expert_ids, gate_values, keep_mask, w_gate, w_up, w_down):
    results = []
    for section in range(SECTIONS):
        tokens_all = states[section]
        mixed = jnp.zeros((TOKENS, D), jnp.float32)
        for expert in range(EXP_WIN):
            chosen = (expert_ids[section] == expert) & (keep_mask[section] == 1)
            picked = jnp.any(chosen, axis=1)
            weight_tok = jnp.sum(jnp.where(chosen, gate_values[section], jnp.zeros_like(gate_values[section])), axis=1)
            index_list = jnp.nonzero(picked, size=N_EP * CAP, fill_value=0)[0].astype(jnp.int32)
            valid = jnp.arange(N_EP * CAP, dtype=jnp.int32) < jnp.sum(picked.astype(jnp.int32))
            rows_sel = tokens_all[index_list]
            result = expert_apply(rows_sel,
                                  w_gate[section][:, expert * FF:(expert + 1) * FF],
                                  w_up[section][:, expert * FF:(expert + 1) * FF],
                                  w_down[section][expert * FF:(expert + 1) * FF, :])
            scale = jnp.where(valid, weight_tok[index_list], jnp.zeros_like(weight_tok[index_list]))
            mixed = mixed.at[index_list].add(scale[:, None] * result)
        results.append(mixed.astype(jnp.bfloat16))
    return jnp.roll(jnp.stack(results), 1, axis=0)
```

```python
import functools

import jax
import jax.numpy as jnp
from jax import lax
from jax.experimental import pallas as pl
from jax.experimental.pallas import tpu as pltpu
from jax.sharding import PartitionSpec as P

EXP_WIN = 2
CAP = 48
CHUNK = 512
RING = 3
GROUP = 4
MESH = pl.DeviceIdType.MESH

A_ME, B_ME, A_Y, B_Y, A_Z, B_Z, A_Q, B_Q = range(8)

(
    X_CROSS, X_AY, X_AZ, X_BY, X_BZ, X_FA, X_FB,
    R_BQ, R_AQ, R_BY, R_AZ, R_SY, R_SZ, R_CROSS, R_OUT,
) = range(15)
KINDS = 15


def moe_kernel(
    chunks, width,
    tab_ref, spread_ref, wcol_ref, states_ref, wg_ref, wu_ref, wd_ref,
    out_ref,
    rows, other, wg_buf, wu_buf, wd_buf, gate, up, hidden, part,
    sum_y, sum_z, sum_b, sum_a, mixed, landed,
    send_sem, recv_sem, wg_sem, wu_sem, wd_sem,
):
    section = lax.axis_index("section")
    ep = lax.axis_index("ep")
    sections = lax.axis_size("section")
    dev_y = (section, ep + 1 - 2 * (ep % 2))
    dev_z = (section, ep + 2 - 4 * ((ep // 2) % 2))
    dev_x = (section, (ep + 4) % 8)
    dev_next = ((section + 1) % sections, ep)
    dev_prev = ((section + sections - 1) % sections, ep)
    units = hidden.shape[1]

    def block(slot):
        return pl.ds(slot * CAP, CAP)

    def copy(kind, k):
        def row(slot):
            return rows.at[k, block(slot)]

        def piece(slot):
            return part.at[k, block(slot)]

        columns = pl.ds(pl.multiple_of(k * width, width), width)
        src, dst, dev = {
            X_CROSS: lambda: (other.at[k], row(B_ME), dev_x),
            X_AY: lambda: (row(A_ME), row(A_Y), dev_y),
            X_AZ: lambda: (row(A_ME), row(A_Z), dev_z),
            X_BY: lambda: (row(B_ME), row(B_Y), dev_y),
            X_BZ: lambda: (row(B_ME), row(B_Z), dev_z),
            X_FA: lambda: (row(A_Y), row(A_Q), dev_z),
            X_FB: lambda: (row(B_Z), row(B_Q), dev_y),
            R_BQ: lambda: (piece(B_Q), landed.at[0, k], dev_y),
            R_AQ: lambda: (piece(A_Q), landed.at[1, k], dev_z),
            R_BY: lambda: (piece(B_Y), landed.at[2, k], dev_y),
            R_AZ: lambda: (piece(A_Z), landed.at[3, k], dev_z),
            R_SY: lambda: (sum_y.at[k], landed.at[4, k], dev_y),
            R_SZ: lambda: (sum_z.at[k], landed.at[5, k], dev_z),
            R_CROSS: lambda: (sum_b.at[k], landed.at[6, k], dev_x),
            R_OUT: lambda: (mixed.at[k], out_ref.at[0, :, columns], dev_next),
        }[kind]()
        return pltpu.make_async_remote_copy(
            src_ref=src,
            dst_ref=dst,
            send_sem=send_sem.at[kind, k],
            recv_sem=recv_sem.at[kind, k],
            device_id=dev,
            device_id_type=MESH,
        )

    def in_weights(k):
        slot = k % RING
        depth = pl.ds(pl.multiple_of(k * width, width), width)
        return (
            pltpu.make_async_copy(wg_ref.at[0, depth], wg_buf.at[slot], wg_sem.at[slot]),
            pltpu.make_async_copy(wu_ref.at[0, depth], wu_buf.at[slot], wu_sem.at[slot]),
        )

    def out_weights(k):
        slot = k % RING
        columns = pl.ds(pl.multiple_of(k * width, width), width)
        return pltpu.make_async_copy(
            wd_ref.at[0, :, columns], wd_buf.at[slot], wd_sem.at[slot]
        )

    for k in range(RING):
        for c in in_weights(k):
            c.start()

    barrier = pltpu.get_barrier_semaphore()
    for dev in (dev_y, dev_z, dev_x, dev_next, dev_prev):
        pl.semaphore_signal(barrier, inc=1, device_id=dev, device_id_type=MESH)

    for k in range(chunks):
        picked = jnp.dot(
            tab_ref[...],
            states_ref[0, :, k * width:(k + 1) * width],
            preferred_element_type=jnp.float32,
        ).astype(jnp.bfloat16)
        rows[k, block(A_ME)] = picked[:CAP]
        other[k] = picked[CAP:]

    pl.semaphore_wait(barrier, 5)

    for k in range(RING):
        out_weights(k).start()

    gate[...] = jnp.zeros_like(gate)
    up[...] = jnp.zeros_like(up)
    tile = min(units, 512)

    def in_step(i, carry):
        @pl.when(i < chunks)
        def _():
            for kind in (X_CROSS, X_AY, X_AZ):
                copy(kind, i).start()

        @pl.when((i >= 2) & (i < chunks + 2))
        def _():
            k = i - 2
            copy(X_CROSS, k).wait_recv()
            copy(X_BZ, k).start()
            copy(X_BY, k).start()
            copy(X_AY, k).wait_recv()
            copy(X_FA, k).start()

        @pl.when((i >= 3) & (i < chunks + 3))
        def _():
            k = i - 3
            copy(X_BZ, k).wait_recv()
            copy(X_FB, k).start()

        @pl.when(i >= 4)
        def _():
            k = i - 4
            for kind in (X_AZ, X_BY, X_FA, X_FB):
                copy(kind, k).wait_recv()
            for c in in_weights(k):
                c.wait()
            slot = k % RING
            for n in range(0, units, tile):
                gate[:, n:n + tile] += jnp.dot(
                    rows[k], wg_buf[slot, :, n:n + tile], preferred_element_type=jnp.float32
                )
                up[:, n:n + tile] += jnp.dot(
                    rows[k], wu_buf[slot, :, n:n + tile], preferred_element_type=jnp.float32
                )

            @pl.when(k + RING < chunks)
            def _():
                for c in in_weights(k + RING):
                    c.start()

        return carry

    lax.fori_loop(0, chunks + 4, in_step, 0)

    def act_step(r, carry):
        at = pl.ds(pl.multiple_of(r * 16, 16), 16)
        g = gate[at]
        hidden[at] = ((g / (1.0 + jnp.exp(-g))) * up[at]).astype(jnp.bfloat16)
        return carry

    lax.fori_loop(0, hidden.shape[0] // 16, act_step, 0)

    def wide(value):
        return value.astype(jnp.float32)

    def out_step(i, carry):
        @pl.when(i < chunks)
        def _():
            out_weights(i).wait()
            part[i] = jnp.dot(
                hidden[...], wd_buf[i % RING], preferred_element_type=jnp.float32
            ).astype(jnp.bfloat16)
            for kind in (R_BQ, R_AQ, R_BY, R_AZ):
                copy(kind, i).start()

            @pl.when(i + RING < chunks)
            def _():
                out_weights(i + RING).start()

            for kind in range(X_CROSS, X_FB + 1):
                copy(kind, i).wait_send()

        @pl.when((i >= 1) & (i < chunks + 1))
        def _():
            k = i - 1
            copy(R_AQ, k).wait_recv()
            sum_y[k] = (wide(part[k, block(A_Y)]) + wide(landed[1, k])).astype(jnp.bfloat16)
            copy(R_SY, k).start()
            copy(R_BQ, k).wait_recv()
            sum_z[k] = (wide(part[k, block(B_Z)]) + wide(landed[0, k])).astype(jnp.bfloat16)
            copy(R_SZ, k).start()

        @pl.when((i >= 2) & (i < chunks + 2))
        def _():
            k = i - 2
            copy(R_BY, k).wait_recv()
            copy(R_SZ, k).wait_recv()
            sum_b[k] = (
                wide(part[k, block(B_ME)]) + wide(landed[2, k]) + wide(landed[5, k])
            ).astype(jnp.bfloat16)
            copy(R_CROSS, k).start()
            copy(R_AZ, k).wait_recv()
            copy(R_SY, k).wait_recv()
            sum_a[k] = wide(part[k, block(A_ME)]) + wide(landed[3, k]) + wide(landed[4, k])

        @pl.when(i >= 4)
        def _():
            k = i - 4
            copy(R_CROSS, k).wait_recv()
            scaled = jnp.concatenate([sum_a[k], wide(landed[6, k])], axis=0) * wcol_ref[...]
            high = scaled.astype(jnp.bfloat16)
            low = (scaled - wide(high)).astype(jnp.bfloat16)
            mixed[k] = jnp.dot(
                spread_ref[...],
                jnp.concatenate([high, low], axis=0),
                preferred_element_type=jnp.float32,
            ).astype(jnp.bfloat16)
            copy(R_OUT, k).start()
            for kind in range(R_BQ, R_CROSS + 1):
                copy(kind, k).wait_send()

        return carry

    lax.fori_loop(0, chunks + 4, out_step, 0)

    def last_step(k, carry):
        copy(R_OUT, k).wait_send()
        copy(R_OUT, k).wait_recv()
        return carry

    lax.fori_loop(0, chunks, last_step, 0)


def moe_call(tab, spread, wcol, states, w_gate, w_up, w_down):
    tokens, model = states.shape[1:]
    units = w_gate.shape[2]
    width = min(CHUNK, model // RING)
    chunks = model // width
    total = 2 * GROUP * CAP
    bf16, f32 = jnp.bfloat16, jnp.float32
    vmem = pl.BlockSpec(memory_space=pltpu.VMEM)
    hbm = pl.BlockSpec(memory_space=pl.ANY)
    return pl.pallas_call(
        functools.partial(moe_kernel, chunks, width),
        out_shape=jax.ShapeDtypeStruct((1, tokens, model), bf16),
        in_specs=[vmem, vmem, vmem, vmem, hbm, hbm, hbm],
        out_specs=hbm,
        scratch_shapes=[
            pltpu.VMEM((chunks, total, width), bf16),
            pltpu.VMEM((chunks, CAP, width), bf16),
            pltpu.VMEM((RING, width, units), bf16),
            pltpu.VMEM((RING, width, units), bf16),
            pltpu.VMEM((RING, units, width), bf16),
            pltpu.VMEM((total, units), f32),
            pltpu.VMEM((total, units), f32),
            pltpu.VMEM((total, units), bf16),
            pltpu.VMEM((chunks, total, width), bf16),
            pltpu.VMEM((chunks, CAP, width), bf16),
            pltpu.VMEM((chunks, CAP, width), bf16),
            pltpu.VMEM((chunks, CAP, width), bf16),
            pltpu.VMEM((chunks, CAP, width), f32),
            pltpu.VMEM((chunks, tokens, width), bf16),
            pltpu.VMEM((7, chunks, CAP, width), bf16),
            pltpu.SemaphoreType.DMA((KINDS, chunks)),
            pltpu.SemaphoreType.DMA((KINDS, chunks)),
            pltpu.SemaphoreType.DMA((RING,)),
            pltpu.SemaphoreType.DMA((RING,)),
            pltpu.SemaphoreType.DMA((RING,)),
        ],
        cost_estimate=pl.CostEstimate(
            flops=6 * total * model * units,
            bytes_accessed=6 * model * units,
            transcendentals=total * units,
        ),
        compiler_params=pltpu.CompilerParams(
            collective_id=0, has_side_effects=True, vmem_limit_bytes=60 * 1024 * 1024
        ),
    )(tab, spread, wcol, states, w_gate, w_up, w_down)


def routing(ids_here, gates_here, keep_here, order):
    chosen = (ids_here[None] == order[:, None, None]) & (keep_here[None] == 1)
    picked = jnp.any(chosen, axis=2)
    weights_tok = jnp.sum(jnp.where(chosen, gates_here[None], 0.0), axis=2)
    slot_index = jnp.cumsum(picked.astype(jnp.int32), axis=1) - 1
    positions = jnp.arange(CAP, dtype=jnp.int32)
    table = (slot_index[:, None, :] == positions[None, :, None]) & picked[:, None, :]
    return table, weights_tok


def grouped_body(states, expert_ids, gate_values, keep_mask, w_gate, w_up, w_down):
    mine = lax.axis_index("ep") // GROUP
    order = jnp.stack([mine, 1 - mine]).astype(jnp.int32)
    table, weights_tok = routing(expert_ids[0], gate_values[0], keep_mask[0], order)
    wcol = jnp.sum(jnp.where(table, weights_tok[:, None, :], 0.0), axis=2)
    tab = table.reshape(EXP_WIN * CAP, -1).astype(jnp.bfloat16)
    spread = jnp.concatenate([tab.T, tab.T], axis=1)
    return moe_call(
        tab, spread, wcol.reshape(EXP_WIN * CAP, 1), states, w_gate, w_up, w_down
    )


def general_body(states, expert_ids, gate_values, keep_mask, w_gate, w_up, w_down):
    slices = lax.axis_size("ep") // EXP_WIN
    order = jnp.arange(EXP_WIN, dtype=jnp.int32)
    table, weights_tok = routing(expert_ids[0], gate_values[0], keep_mask[0], order)
    compact = jnp.einsum(
        "ect,td->ecd",
        table.astype(jnp.bfloat16),
        states[0],
        preferred_element_type=jnp.float32,
    ).astype(jnp.bfloat16)
    arrived = lax.all_to_all(
        jnp.repeat(compact, slices, axis=0), "ep", split_axis=0, concat_axis=0, tiled=True
    )
    flat = arrived.reshape(-1, arrived.shape[2])
    gate = jnp.dot(flat, w_gate[0], preferred_element_type=jnp.float32)
    up = jnp.dot(flat, w_up[0], preferred_element_type=jnp.float32)
    hidden = (jax.nn.silu(gate) * up).astype(jnp.bfloat16)
    piece = jnp.dot(hidden, w_down[0], preferred_element_type=jnp.float32).astype(jnp.bfloat16)
    returned = lax.all_to_all(
        piece.reshape(arrived.shape), "ep", split_axis=0, concat_axis=0, tiled=True
    )
    expert_out = jnp.sum(
        returned.reshape(EXP_WIN, slices, CAP, -1).astype(jnp.float32), axis=1
    )
    combine = table.astype(jnp.float32) * weights_tok[:, None, :]
    mixed = jnp.einsum("ect,ecd->td", combine, expert_out, precision=lax.Precision.HIGHEST)
    sections = lax.axis_size("section")
    return lax.ppermute(
        mixed.astype(jnp.bfloat16)[None],
        "section",
        [(i, (i + 1) % sections) for i in range(sections)],
    )


def solution(mesh):
    grouped = mesh.shape["ep"] == EXP_WIN * GROUP and mesh.shape["section"] > 2
    return jax.shard_map(
        grouped_body if grouped else general_body,
        mesh=mesh,
        in_specs=(
            P("section", "ep", None),
            P("section", "ep", None),
            P("section", "ep", None),
            P("section", "ep", None),
            P("section", None, "ep"),
            P("section", None, "ep"),
            P("section", "ep", None),
        ),
        out_specs=P("section", "ep", None),
        check_vma=False,
    )
```

```python
import functools

import jax
import jax.numpy as jnp
from jax import lax
from jax.experimental import pallas as pl
from jax.experimental.pallas import tpu as pltpu
from jax.sharding import PartitionSpec as P

EXP_WIN = 2
CAP = 48
CHUNK = 512
RING = 3
LANES = 128
GROUP = 4
MESH = pl.DeviceIdType.MESH

A_ME, B_ME, A_Y, B_Y, A_Z, B_Z, A_Q, B_Q = range(8)

(
    X_CROSS, X_AY, X_AZ, X_BY, X_BZ, X_FA, X_FB,
    R_BQ, R_AQ, R_BY, R_AZ, R_SY, R_SZ, R_CROSS, R_OUT,
) = range(15)
KINDS = 15


def moe_kernel(
    chunks, width,
    ids_ref, gates_ref, keep_ref, states_ref, wg_ref, wu_ref, wd_ref,
    out_ref,
    tab, spread, wcol,
    rows, other, wg_buf, wu_buf, wd_buf, gate, up, hidden, part,
    sum_y, sum_z, sum_b, sum_a, mixed, landed,
    send_sem, recv_sem, wg_sem, wu_sem, wd_sem,
):
    section = lax.axis_index("section")
    ep = lax.axis_index("ep")
    sections = lax.axis_size("section")
    ep_y = ep + 1 - 2 * (ep % 2)
    ep_z = ep + 2 - 4 * ((ep // 2) % 2)
    dev_y = (section, ep_y)
    dev_z = (section, ep_z)
    dev_x = (section, (ep + 4) % 8)
    dev_next = ((section + 1) % sections, ep)
    dev_prev = ((section + sections - 1) % sections, ep)
    units = hidden.shape[1]

    def block(slot):
        return pl.ds(pl.multiple_of(slot * CAP, 16), CAP)

    def z_then_y(k):
        return (section, ep_z + (k % 2) * (ep_y - ep_z))

    def y_then_z(k):
        return (section, ep_y + (k % 2) * (ep_z - ep_y))

    def y_then_z_slot(k):
        return A_Y + (k % 2) * (A_Z - A_Y)

    def z_then_y_slot(k):
        return A_Z + (k % 2) * (A_Y - A_Z)

    def copy(kind, k):
        def row(slot):
            return rows.at[k, block(slot)]

        def piece(slot):
            return part.at[k, block(slot)]

        columns = pl.ds(pl.multiple_of(k * width, width), width)
        src, dst, dev = {
            X_CROSS: lambda: (other.at[k], row(B_ME), dev_x),
            X_AY: lambda: (row(A_ME), row(A_Y), dev_y),
            X_AZ: lambda: (row(A_ME), row(A_Z), dev_z),
            X_BY: lambda: (row(B_ME), row(B_Y), dev_y),
            X_BZ: lambda: (row(B_ME), row(B_Z), dev_z),
            X_FA: lambda: (row(y_then_z_slot(k)), row(A_Q), z_then_y(k)),
            X_FB: lambda: (row(B_Z), row(B_Q), dev_y),
            R_BQ: lambda: (piece(B_Q), landed.at[0, k], dev_y),
            R_AQ: lambda: (piece(A_Q), landed.at[1, k], z_then_y(k)),
            R_BY: lambda: (piece(B_Y), landed.at[2, k], dev_y),
            R_AZ: lambda: (piece(z_then_y_slot(k)), landed.at[3, k], z_then_y(k)),
            R_SY: lambda: (sum_y.at[k], landed.at[4, k], y_then_z(k)),
            R_SZ: lambda: (sum_z.at[k], landed.at[5, k], dev_z),
            R_CROSS: lambda: (sum_b.at[k], landed.at[6, k], dev_x),
            R_OUT: lambda: (mixed.at[k], out_ref.at[0, :, columns], dev_next),
        }[kind]()
        return pltpu.make_async_remote_copy(
            src_ref=src,
            dst_ref=dst,
            send_sem=send_sem.at[kind, k],
            recv_sem=recv_sem.at[kind, k],
            device_id=dev,
            device_id_type=MESH,
        )

    def in_weights(k):
        slot = k % RING
        depth = pl.ds(pl.multiple_of(k * width, width), width)
        return (
            pltpu.make_async_copy(wg_ref.at[0, depth], wg_buf.at[slot], wg_sem.at[slot]),
            pltpu.make_async_copy(wu_ref.at[0, depth], wu_buf.at[slot], wu_sem.at[slot]),
        )

    def out_weights(k):
        slot = k % RING
        columns = pl.ds(pl.multiple_of(k * width, width), width)
        return pltpu.make_async_copy(
            wd_ref.at[0, :, columns], wd_buf.at[slot], wd_sem.at[slot]
        )

    for k in range(RING):
        for c in in_weights(k):
            c.start()

    barrier = pltpu.get_barrier_semaphore()
    for dev in (dev_y, dev_z, dev_x, dev_next, dev_prev):
        pl.semaphore_signal(barrier, inc=1, device_id=dev, device_id_type=MESH)

    tokens = states_ref.shape[1]
    mine = ep // GROUP

    def choice(expert):
        chosen = (ids_ref[0] == expert) & (keep_ref[0] == 1)
        picked = jnp.sum(jnp.where(chosen, 1.0, 0.0), axis=0, keepdims=True)
        weight = jnp.sum(jnp.where(chosen, gates_ref[0], 0.0), axis=0, keepdims=True)
        return picked, weight

    picked_own, weight_own = choice(mine)
    picked_other, weight_other = choice(1 - mine)
    before = lax.broadcasted_iota(jnp.int32, (tokens, tokens), 0)
    token = lax.broadcasted_iota(jnp.int32, (tokens, tokens), 1)
    slot_row = lax.broadcasted_iota(jnp.int32, (LANES, tokens), 0)
    own = slot_row < CAP
    picked = jnp.where(own, picked_own, jnp.where(slot_row < 2 * CAP, picked_other, 0.0))
    rank = jnp.dot(
        picked.astype(jnp.bfloat16),
        jnp.where(before <= token, 1.0, 0.0).astype(jnp.bfloat16),
        preferred_element_type=jnp.float32,
    )
    place = jnp.where(own, slot_row, slot_row - CAP).astype(jnp.float32)
    table = jnp.where((picked > 0.5) & (rank - 1.0 == place), 1.0, 0.0)
    tab[...] = table.astype(jnp.bfloat16)
    wcol[...] = jnp.sum(
        table * jnp.where(own, weight_own, weight_other), axis=1, keepdims=True
    )
    across = jnp.transpose(table).astype(jnp.bfloat16)
    spread[:, :LANES] = across
    spread[:, LANES:] = across

    def gather(k):
        columns = pl.ds(pl.multiple_of(k * width, width), width)
        taken = jnp.dot(
            tab[: 2 * CAP], states_ref[0, :, columns], preferred_element_type=jnp.float32
        ).astype(jnp.bfloat16)
        rows[k, block(A_ME)] = taken[:CAP]
        other[k] = taken[CAP:]

    for k in range(2):
        gather(k)

    pl.semaphore_wait(barrier, 5)

    for k in range(RING):
        out_weights(k).start()

    gate[...] = jnp.zeros_like(gate)
    up[...] = jnp.zeros_like(up)
    tile = min(units, 512)

    def arrived(k):
        for kind in (X_BY, X_FA, X_FB):
            copy(kind, k).wait_recv()
        for c in in_weights(k):
            c.wait()

    def in_step(i, carry):
        @pl.when(i < chunks)
        def _():
            for kind in (X_CROSS, X_AY, X_AZ):
                copy(kind, i).start()

        @pl.when(i + 2 < chunks)
        def _():
            gather(i + 2)

        @pl.when((i >= 2) & (i < chunks + 2))
        def _():
            k = i - 2
            copy(X_CROSS, k).wait_recv()
            copy(X_BZ, k).start()
            copy(X_BY, k).start()
            copy(X_AY, k).wait_recv()
            copy(X_AZ, k).wait_recv()
            copy(X_FA, k).start()

        @pl.when((i >= 3) & (i < chunks + 3))
        def _():
            k = i - 3
            copy(X_BZ, k).wait_recv()
            copy(X_FB, k).start()

        @pl.when(i >= 4)
        def _():
            k = i - 4
            arrived(k)
            slot = k % RING
            for n in range(0, units, tile):
                gate[:, n:n + tile] += jnp.dot(
                    rows[k], wg_buf[slot, :, n:n + tile], preferred_element_type=jnp.float32
                )
                up[:, n:n + tile] += jnp.dot(
                    rows[k], wu_buf[slot, :, n:n + tile], preferred_element_type=jnp.float32
                )

            @pl.when(k + RING < chunks)
            def _():
                for c in in_weights(k + RING):
                    c.start()

        return carry

    lax.fori_loop(0, chunks + 3, in_step, 0)

    last = chunks - 1
    arrived(last)
    tile = min(units, 256)
    for n in range(0, units, tile):
        at = slice(n, n + tile)
        g = gate[:, at] + jnp.dot(
            rows[last], wg_buf[last % RING, :, at], preferred_element_type=jnp.float32
        )
        u = up[:, at] + jnp.dot(
            rows[last], wu_buf[last % RING, :, at], preferred_element_type=jnp.float32
        )
        hidden[:, at] = ((g / (1.0 + jnp.exp(-g))) * u).astype(jnp.bfloat16)

    def wide(value):
        return value.astype(jnp.float32)

    def out_step(i, carry):
        @pl.when(i < chunks)
        def _():
            out_weights(i).wait()
            part[i] = jnp.dot(
                hidden[...], wd_buf[i % RING], preferred_element_type=jnp.float32
            ).astype(jnp.bfloat16)
            for kind in (R_BQ, R_AQ, R_BY, R_AZ):
                copy(kind, i).start()

            @pl.when(i + RING < chunks)
            def _():
                out_weights(i + RING).start()

            for kind in range(X_CROSS, X_FB + 1):
                copy(kind, i).wait_send()

        @pl.when((i >= 1) & (i < chunks + 1))
        def _():
            k = i - 1
            copy(R_AQ, k).wait_recv()
            sum_y[k] = (wide(part[k, block(y_then_z_slot(k))]) + wide(landed[1, k])).astype(jnp.bfloat16)
            copy(R_SY, k).start()
            copy(R_BQ, k).wait_recv()
            sum_z[k] = (wide(part[k, block(B_Z)]) + wide(landed[0, k])).astype(jnp.bfloat16)
            copy(R_SZ, k).start()

        @pl.when((i >= 2) & (i < chunks + 2))
        def _():
            k = i - 2
            copy(R_BY, k).wait_recv()
            copy(R_SZ, k).wait_recv()
            sum_b[k] = (
                wide(part[k, block(B_ME)]) + wide(landed[2, k]) + wide(landed[5, k])
            ).astype(jnp.bfloat16)
            copy(R_CROSS, k).start()
            copy(R_AZ, k).wait_recv()
            copy(R_SY, k).wait_recv()
            sum_a[k] = wide(part[k, block(A_ME)]) + wide(landed[3, k]) + wide(landed[4, k])

        @pl.when(i >= 4)
        def _():
            k = i - 4
            copy(R_CROSS, k).wait_recv()
            unused = jnp.zeros((LANES - 2 * CAP, width), jnp.float32)
            values = jnp.concatenate([sum_a[k], wide(landed[6, k]), unused], axis=0)
            scaled = values * wcol[...]
            high = scaled.astype(jnp.bfloat16)
            low = (scaled - wide(high)).astype(jnp.bfloat16)
            mixed[k] = jnp.dot(
                spread[...],
                jnp.concatenate([high, low], axis=0),
                preferred_element_type=jnp.float32,
            ).astype(jnp.bfloat16)
            copy(R_OUT, k).start()
            for kind in range(R_BQ, R_CROSS + 1):
                copy(kind, k).wait_send()

        return carry

    lax.fori_loop(0, chunks + 4, out_step, 0)

    def last_step(k, carry):
        copy(R_OUT, k).wait_send()
        copy(R_OUT, k).wait_recv()
        return carry

    lax.fori_loop(0, chunks, last_step, 0)


def moe_call(expert_ids, gate_values, keep_mask, states, w_gate, w_up, w_down):
    tokens, model = states.shape[1:]
    units = w_gate.shape[2]
    width = min(CHUNK, model // RING)
    chunks = model // width
    total = 2 * GROUP * CAP
    bf16, f32 = jnp.bfloat16, jnp.float32
    vmem = pl.BlockSpec(memory_space=pltpu.VMEM)
    hbm = pl.BlockSpec(memory_space=pl.ANY)
    return pl.pallas_call(
        functools.partial(moe_kernel, chunks, width),
        out_shape=jax.ShapeDtypeStruct((1, tokens, model), bf16),
        in_specs=[vmem, vmem, vmem, vmem, hbm, hbm, hbm],
        out_specs=hbm,
        scratch_shapes=[
            pltpu.VMEM((LANES, tokens), bf16),
            pltpu.VMEM((tokens, 2 * LANES), bf16),
            pltpu.VMEM((LANES, 1), f32),
            pltpu.VMEM((chunks, total, width), bf16),
            pltpu.VMEM((chunks, CAP, width), bf16),
            pltpu.VMEM((RING, width, units), bf16),
            pltpu.VMEM((RING, width, units), bf16),
            pltpu.VMEM((RING, units, width), bf16),
            pltpu.VMEM((total, units), f32),
            pltpu.VMEM((total, units), f32),
            pltpu.VMEM((total, units), bf16),
            pltpu.VMEM((chunks, total, width), bf16),
            pltpu.VMEM((chunks, CAP, width), bf16),
            pltpu.VMEM((chunks, CAP, width), bf16),
            pltpu.VMEM((chunks, CAP, width), bf16),
            pltpu.VMEM((chunks, CAP, width), f32),
            pltpu.VMEM((chunks, tokens, width), bf16),
            pltpu.VMEM((7, chunks, CAP, width), bf16),
            pltpu.SemaphoreType.DMA((KINDS, chunks)),
            pltpu.SemaphoreType.DMA((KINDS, chunks)),
            pltpu.SemaphoreType.DMA((RING,)),
            pltpu.SemaphoreType.DMA((RING,)),
            pltpu.SemaphoreType.DMA((RING,)),
        ],
        cost_estimate=pl.CostEstimate(
            flops=6 * total * model * units,
            bytes_accessed=6 * model * units,
            transcendentals=total * units,
        ),
        compiler_params=pltpu.CompilerParams(
            collective_id=0, has_side_effects=True, vmem_limit_bytes=60 * 1024 * 1024
        ),
    )(expert_ids, gate_values, keep_mask, states, w_gate, w_up, w_down)


def routing(ids_here, gates_here, keep_here, order):
    chosen = (ids_here[None] == order[:, None, None]) & (keep_here[None] == 1)
    picked = jnp.any(chosen, axis=2)
    weights_tok = jnp.sum(jnp.where(chosen, gates_here[None], 0.0), axis=2)
    slot_index = jnp.cumsum(picked.astype(jnp.int32), axis=1) - 1
    positions = jnp.arange(CAP, dtype=jnp.int32)
    table = (slot_index[:, None, :] == positions[None, :, None]) & picked[:, None, :]
    return table, weights_tok


def grouped_body(states, expert_ids, gate_values, keep_mask, w_gate, w_up, w_down):
    expert_ids, gate_values, keep_mask = (
        jnp.swapaxes(value, 1, 2) for value in (expert_ids, gate_values, keep_mask)
    )
    return moe_call(expert_ids, gate_values, keep_mask, states, w_gate, w_up, w_down)


def general_body(states, expert_ids, gate_values, keep_mask, w_gate, w_up, w_down):
    slices = lax.axis_size("ep") // EXP_WIN
    order = jnp.arange(EXP_WIN, dtype=jnp.int32)
    table, weights_tok = routing(expert_ids[0], gate_values[0], keep_mask[0], order)
    compact = jnp.einsum(
        "ect,td->ecd",
        table.astype(jnp.bfloat16),
        states[0],
        preferred_element_type=jnp.float32,
    ).astype(jnp.bfloat16)
    arrived = lax.all_to_all(
        jnp.repeat(compact, slices, axis=0), "ep", split_axis=0, concat_axis=0, tiled=True
    )
    flat = arrived.reshape(-1, arrived.shape[2])
    gate = jnp.dot(flat, w_gate[0], preferred_element_type=jnp.float32)
    up = jnp.dot(flat, w_up[0], preferred_element_type=jnp.float32)
    hidden = (jax.nn.silu(gate) * up).astype(jnp.bfloat16)
    piece = jnp.dot(hidden, w_down[0], preferred_element_type=jnp.float32).astype(jnp.bfloat16)
    returned = lax.all_to_all(
        piece.reshape(arrived.shape), "ep", split_axis=0, concat_axis=0, tiled=True
    )
    expert_out = jnp.sum(
        returned.reshape(EXP_WIN, slices, CAP, -1).astype(jnp.float32), axis=1
    )
    combine = table.astype(jnp.float32) * weights_tok[:, None, :]
    mixed = jnp.einsum("ect,ecd->td", combine, expert_out, precision=lax.Precision.HIGHEST)
    sections = lax.axis_size("section")
    return lax.ppermute(
        mixed.astype(jnp.bfloat16)[None],
        "section",
        [(i, (i + 1) % sections) for i in range(sections)],
    )


def solution(mesh):
    grouped = mesh.shape["ep"] == EXP_WIN * GROUP and mesh.shape["section"] > 2
    return jax.shard_map(
        grouped_body if grouped else general_body,
        mesh=mesh,
        in_specs=(
            P("section", "ep", None),
            P("section", "ep", None),
            P("section", "ep", None),
            P("section", "ep", None),
            P("section", None, "ep"),
            P("section", None, "ep"),
            P("section", "ep", None),
        ),
        out_specs=P("section", "ep", None),
        check_vma=False,
    )
```

```python
import functools

import jax
import jax.numpy as jnp
from jax import lax
from jax.experimental import pallas as pl
from jax.experimental.pallas import tpu as pltpu
from jax.sharding import PartitionSpec as P

EXP_WIN = 2
CAP = 48
CHUNK = 512
RING = 3
LANES = 128
GROUP = 4
MESH = pl.DeviceIdType.MESH

A_ME, B_ME, A_Y, B_Y, A_Z, B_Z, A_Q, B_Q = range(8)

(
    X_CROSS, X_AY, X_AZ, X_BY, X_BZ, X_FA, X_FB,
    R_BQ, R_AQ, R_BY, R_AZ, R_SY, R_SZ, R_CROSS, R_OUT,
) = range(15)
KINDS = 15


def moe_kernel(
    chunks, width,
    ids_hbm, gates_hbm, keep_hbm, states_hbm, wg_ref, wu_ref, wd_ref,
    out_ref,
    ids_ref, gates_ref, keep_ref, states_ref, tab, spread, wcol,
    rows, other, wg_buf, wu_buf, wd_buf, gate, up, hidden, part,
    sum_y, sum_z, sum_b, sum_a, mixed, landed,
    send_sem, recv_sem, wg_sem, wu_sem, wd_sem, load_sem,
):
    section = lax.axis_index("section")
    ep = lax.axis_index("ep")
    sections = lax.axis_size("section")
    ep_y = ep + 1 - 2 * (ep % 2)
    ep_z = ep + 2 - 4 * ((ep // 2) % 2)
    dev_y = (section, ep_y)
    dev_z = (section, ep_z)
    dev_x = (section, (ep + 4) % 8)
    dev_next = ((section + 1) % sections, ep)
    dev_prev = ((section + sections - 1) % sections, ep)
    units = hidden.shape[1]

    def block(slot):
        return pl.ds(pl.multiple_of(slot * CAP, 16), CAP)

    def z_then_y(k):
        return (section, ep_z + (k % 2) * (ep_y - ep_z))

    def y_then_z(k):
        return (section, ep_y + (k % 2) * (ep_z - ep_y))

    def y_then_z_slot(k):
        return A_Y + (k % 2) * (A_Z - A_Y)

    def z_then_y_slot(k):
        return A_Z + (k % 2) * (A_Y - A_Z)

    def copy(kind, k):
        def row(slot):
            return rows.at[k, block(slot)]

        def piece(slot):
            return part.at[k, block(slot)]

        columns = pl.ds(pl.multiple_of(k * width, width), width)
        src, dst, dev = {
            X_CROSS: lambda: (other.at[k], row(B_ME), dev_x),
            X_AY: lambda: (row(A_ME), row(A_Y), dev_y),
            X_AZ: lambda: (row(A_ME), row(A_Z), dev_z),
            X_BY: lambda: (row(B_ME), row(B_Y), dev_y),
            X_BZ: lambda: (row(B_ME), row(B_Z), dev_z),
            X_FA: lambda: (row(y_then_z_slot(k)), row(A_Q), z_then_y(k)),
            X_FB: lambda: (row(B_Z), row(B_Q), dev_y),
            R_BQ: lambda: (piece(B_Q), landed.at[0, k], dev_y),
            R_AQ: lambda: (piece(A_Q), landed.at[1, k], z_then_y(k)),
            R_BY: lambda: (piece(B_Y), landed.at[2, k], dev_y),
            R_AZ: lambda: (piece(z_then_y_slot(k)), landed.at[3, k], z_then_y(k)),
            R_SY: lambda: (sum_y.at[k], landed.at[4, k], y_then_z(k)),
            R_SZ: lambda: (sum_z.at[k], landed.at[5, k], dev_z),
            R_CROSS: lambda: (sum_b.at[k], landed.at[6, k], dev_x),
            R_OUT: lambda: (mixed.at[k], out_ref.at[0, :, columns], dev_next),
        }[kind]()
        return pltpu.make_async_remote_copy(
            src_ref=src,
            dst_ref=dst,
            send_sem=send_sem.at[kind, k],
            recv_sem=recv_sem.at[kind, k],
            device_id=dev,
            device_id_type=MESH,
        )

    def in_weights(k):
        slot = k % RING
        depth = pl.ds(pl.multiple_of(k * width, width), width)
        return (
            pltpu.make_async_copy(wg_ref.at[0, depth], wg_buf.at[slot], wg_sem.at[slot]),
            pltpu.make_async_copy(wu_ref.at[0, depth], wu_buf.at[slot], wu_sem.at[slot]),
        )

    def out_weights(k):
        slot = k % RING
        columns = pl.ds(pl.multiple_of(k * width, width), width)
        return pltpu.make_async_copy(
            wd_ref.at[0, :, columns], wd_buf.at[slot], wd_sem.at[slot]
        )

    loads = [
        pltpu.make_async_copy(src, dst, load_sem.at[n])
        for n, (src, dst) in enumerate((
            (ids_hbm, ids_ref),
            (gates_hbm, gates_ref),
            (keep_hbm, keep_ref),
            (states_hbm, states_ref),
        ))
    ]
    for load in loads:
        load.start()
    for k in range(RING):
        for c in in_weights(k):
            c.start()

    barrier = pltpu.get_barrier_semaphore()
    for dev in (dev_y, dev_z, dev_x, dev_next, dev_prev):
        pl.semaphore_signal(barrier, inc=1, device_id=dev, device_id_type=MESH)

    for load in loads[:3]:
        load.wait()

    tokens = states_ref.shape[1]
    mine = ep // GROUP

    def choice(expert):
        chosen = (ids_ref[0] == expert) & (keep_ref[0] == 1)
        picked = jnp.sum(jnp.where(chosen, 1.0, 0.0), axis=0, keepdims=True)
        weight = jnp.sum(jnp.where(chosen, gates_ref[0], 0.0), axis=0, keepdims=True)
        return picked, weight

    picked_own, weight_own = choice(mine)
    picked_other, weight_other = choice(1 - mine)
    before = lax.broadcasted_iota(jnp.int32, (tokens, tokens), 0)
    token = lax.broadcasted_iota(jnp.int32, (tokens, tokens), 1)
    slot_row = lax.broadcasted_iota(jnp.int32, (LANES, tokens), 0)
    own = slot_row < CAP
    picked = jnp.where(own, picked_own, jnp.where(slot_row < 2 * CAP, picked_other, 0.0))
    rank = jnp.dot(
        picked.astype(jnp.bfloat16),
        jnp.where(before <= token, 1.0, 0.0).astype(jnp.bfloat16),
        preferred_element_type=jnp.float32,
    )
    place = jnp.where(own, slot_row, slot_row - CAP).astype(jnp.float32)
    table = jnp.where((picked > 0.5) & (rank - 1.0 == place), 1.0, 0.0)
    tab[...] = table.astype(jnp.bfloat16)
    wcol[...] = jnp.sum(
        table * jnp.where(own, weight_own, weight_other), axis=1, keepdims=True
    )
    across = jnp.transpose(table).astype(jnp.bfloat16)
    spread[:, :LANES] = across
    spread[:, LANES:] = across

    def gather(k):
        columns = pl.ds(pl.multiple_of(k * width, width), width)
        taken = jnp.dot(
            tab[: 2 * CAP], states_ref[0, :, columns], preferred_element_type=jnp.float32
        ).astype(jnp.bfloat16)
        rows[k, block(A_ME)] = taken[:CAP]
        other[k] = taken[CAP:]

    loads[3].wait()
    gather(0)
    pl.semaphore_wait(barrier, 5)
    copy(X_CROSS, 0).start()
    for k in range(1, 3):
        gather(k)

    for k in range(RING):
        out_weights(k).start()

    gate[...] = jnp.zeros_like(gate)
    up[...] = jnp.zeros_like(up)
    tile = min(units, 512)

    def arrived(k):
        for kind in (X_BY, X_FA, X_FB):
            copy(kind, k).wait_recv()
        for c in in_weights(k):
            c.wait()

    def in_step(i, carry):
        @pl.when(i < chunks)
        def _():
            @pl.when(i + 1 < chunks)
            def _():
                copy(X_CROSS, i + 1).start()

            copy(X_AY, i).start()
            copy(X_AZ, i).start()

        @pl.when(i + 3 < chunks)
        def _():
            gather(i + 3)

        @pl.when((i >= 2) & (i < chunks + 2))
        def _():
            k = i - 2
            copy(X_CROSS, k).wait_recv()
            copy(X_BZ, k).start()
            copy(X_BY, k).start()
            copy(X_AY, k).wait_recv()
            copy(X_AZ, k).wait_recv()
            copy(X_FA, k).start()

        @pl.when((i >= 3) & (i < chunks + 3))
        def _():
            k = i - 3
            copy(X_BZ, k).wait_recv()
            copy(X_FB, k).start()

        @pl.when(i >= 4)
        def _():
            k = i - 4
            arrived(k)
            slot = k % RING
            for n in range(0, units, tile):
                gate[:, n:n + tile] += jnp.dot(
                    rows[k], wg_buf[slot, :, n:n + tile], preferred_element_type=jnp.float32
                )
                up[:, n:n + tile] += jnp.dot(
                    rows[k], wu_buf[slot, :, n:n + tile], preferred_element_type=jnp.float32
                )

            @pl.when(k + RING < chunks)
            def _():
                for c in in_weights(k + RING):
                    c.start()

        return carry

    lax.fori_loop(0, chunks + 3, in_step, 0)

    last = chunks - 1
    arrived(last)
    tile = min(units, 256)
    for n in range(0, units, tile):
        at = slice(n, n + tile)
        g = gate[:, at] + jnp.dot(
            rows[last], wg_buf[last % RING, :, at], preferred_element_type=jnp.float32
        )
        u = up[:, at] + jnp.dot(
            rows[last], wu_buf[last % RING, :, at], preferred_element_type=jnp.float32
        )
        hidden[:, at] = ((g / (1.0 + jnp.exp(-g))) * u).astype(jnp.bfloat16)

    def wide(value):
        return value.astype(jnp.float32)

    def out_step(i, carry):
        @pl.when(i < chunks)
        def _():
            out_weights(i).wait()
            part[i] = jnp.dot(
                hidden[...], wd_buf[i % RING], preferred_element_type=jnp.float32
            ).astype(jnp.bfloat16)
            for kind in (R_BQ, R_AQ, R_BY, R_AZ):
                copy(kind, i).start()

            @pl.when(i + RING < chunks)
            def _():
                out_weights(i + RING).start()

            for kind in range(X_CROSS, X_FB + 1):
                copy(kind, i).wait_send()

        @pl.when((i >= 2) & (i < chunks + 2))
        def _():
            k = i - 2
            copy(R_AQ, k).wait_recv()
            sum_y[k] = (wide(part[k, block(y_then_z_slot(k))]) + wide(landed[1, k])).astype(jnp.bfloat16)
            copy(R_SY, k).start()
            copy(R_BQ, k).wait_recv()
            sum_z[k] = (wide(part[k, block(B_Z)]) + wide(landed[0, k])).astype(jnp.bfloat16)
            copy(R_SZ, k).start()

        @pl.when((i >= 3) & (i < chunks + 3))
        def _():
            k = i - 3
            copy(R_BY, k).wait_recv()
            copy(R_SZ, k).wait_recv()
            sum_b[k] = (
                wide(part[k, block(B_ME)]) + wide(landed[2, k]) + wide(landed[5, k])
            ).astype(jnp.bfloat16)
            copy(R_CROSS, k).start()
            copy(R_AZ, k).wait_recv()
            copy(R_SY, k).wait_recv()
            sum_a[k] = wide(part[k, block(A_ME)]) + wide(landed[3, k]) + wide(landed[4, k])

        @pl.when(i >= 5)
        def _():
            k = i - 5
            copy(R_CROSS, k).wait_recv()
            unused = jnp.zeros((LANES - 2 * CAP, width), jnp.float32)
            values = jnp.concatenate([sum_a[k], wide(landed[6, k]), unused], axis=0)
            scaled = values * wcol[...]
            high = scaled.astype(jnp.bfloat16)
            low = (scaled - wide(high)).astype(jnp.bfloat16)
            mixed[k] = jnp.dot(
                spread[...],
                jnp.concatenate([high, low], axis=0),
                preferred_element_type=jnp.float32,
            ).astype(jnp.bfloat16)
            copy(R_OUT, k).start()
            for kind in range(R_BQ, R_CROSS + 1):
                copy(kind, k).wait_send()

        return carry

    lax.fori_loop(0, chunks + 5, out_step, 0)

    def last_step(k, carry):
        copy(R_OUT, k).wait_send()
        copy(R_OUT, k).wait_recv()
        return carry

    lax.fori_loop(0, chunks, last_step, 0)


def moe_call(expert_ids, gate_values, keep_mask, states, w_gate, w_up, w_down):
    tokens, model = states.shape[1:]
    units = w_gate.shape[2]
    width = min(CHUNK, model // RING)
    chunks = model // width
    total = 2 * GROUP * CAP
    bf16, f32 = jnp.bfloat16, jnp.float32
    hbm = pl.BlockSpec(memory_space=pltpu.HBM)
    return pl.pallas_call(
        functools.partial(moe_kernel, chunks, width),
        out_shape=jax.ShapeDtypeStruct((1, tokens, model), bf16),
        in_specs=[hbm] * 7,
        out_specs=pl.BlockSpec(memory_space=pl.ANY),
        scratch_shapes=[
            pltpu.VMEM((1, 2, tokens), jnp.int32),
            pltpu.VMEM((1, 2, tokens), f32),
            pltpu.VMEM((1, 2, tokens), jnp.int32),
            pltpu.VMEM((1, tokens, model), bf16),
            pltpu.VMEM((LANES, tokens), bf16),
            pltpu.VMEM((tokens, 2 * LANES), bf16),
            pltpu.VMEM((LANES, 1), f32),
            pltpu.VMEM((chunks, total, width), bf16),
            pltpu.VMEM((chunks, CAP, width), bf16),
            pltpu.VMEM((RING, width, units), bf16),
            pltpu.VMEM((RING, width, units), bf16),
            pltpu.VMEM((RING, units, width), bf16),
            pltpu.VMEM((total, units), f32),
            pltpu.VMEM((total, units), f32),
            pltpu.VMEM((total, units), bf16),
            pltpu.VMEM((chunks, total, width), bf16),
            pltpu.VMEM((chunks, CAP, width), bf16),
            pltpu.VMEM((chunks, CAP, width), bf16),
            pltpu.VMEM((chunks, CAP, width), bf16),
            pltpu.VMEM((chunks, CAP, width), f32),
            pltpu.VMEM((chunks, tokens, width), bf16),
            pltpu.VMEM((7, chunks, CAP, width), bf16),
            pltpu.SemaphoreType.DMA((KINDS, chunks)),
            pltpu.SemaphoreType.DMA((KINDS, chunks)),
            pltpu.SemaphoreType.DMA((RING,)),
            pltpu.SemaphoreType.DMA((RING,)),
            pltpu.SemaphoreType.DMA((RING,)),
            pltpu.SemaphoreType.DMA((4,)),
        ],
        cost_estimate=pl.CostEstimate(
            flops=6 * total * model * units,
            bytes_accessed=6 * model * units,
            transcendentals=total * units,
        ),
        compiler_params=pltpu.CompilerParams(
            collective_id=0, has_side_effects=True, vmem_limit_bytes=60 * 1024 * 1024
        ),
    )(expert_ids, gate_values, keep_mask, states, w_gate, w_up, w_down)


def routing(ids_here, gates_here, keep_here, order):
    chosen = (ids_here[None] == order[:, None, None]) & (keep_here[None] == 1)
    picked = jnp.any(chosen, axis=2)
    weights_tok = jnp.sum(jnp.where(chosen, gates_here[None], 0.0), axis=2)
    slot_index = jnp.cumsum(picked.astype(jnp.int32), axis=1) - 1
    positions = jnp.arange(CAP, dtype=jnp.int32)
    table = (slot_index[:, None, :] == positions[None, :, None]) & picked[:, None, :]
    return table, weights_tok


def grouped_body(states, expert_ids, gate_values, keep_mask, w_gate, w_up, w_down):
    expert_ids, gate_values, keep_mask = (
        jnp.swapaxes(value, 1, 2) for value in (expert_ids, gate_values, keep_mask)
    )
    return moe_call(expert_ids, gate_values, keep_mask, states, w_gate, w_up, w_down)


def general_body(states, expert_ids, gate_values, keep_mask, w_gate, w_up, w_down):
    slices = lax.axis_size("ep") // EXP_WIN
    order = jnp.arange(EXP_WIN, dtype=jnp.int32)
    table, weights_tok = routing(expert_ids[0], gate_values[0], keep_mask[0], order)
    compact = jnp.einsum(
        "ect,td->ecd",
        table.astype(jnp.bfloat16),
        states[0],
        preferred_element_type=jnp.float32,
    ).astype(jnp.bfloat16)
    arrived = lax.all_to_all(
        jnp.repeat(compact, slices, axis=0), "ep", split_axis=0, concat_axis=0, tiled=True
    )
    flat = arrived.reshape(-1, arrived.shape[2])
    gate = jnp.dot(flat, w_gate[0], preferred_element_type=jnp.float32)
    up = jnp.dot(flat, w_up[0], preferred_element_type=jnp.float32)
    hidden = (jax.nn.silu(gate) * up).astype(jnp.bfloat16)
    piece = jnp.dot(hidden, w_down[0], preferred_element_type=jnp.float32).astype(jnp.bfloat16)
    returned = lax.all_to_all(
        piece.reshape(arrived.shape), "ep", split_axis=0, concat_axis=0, tiled=True
    )
    expert_out = jnp.sum(
        returned.reshape(EXP_WIN, slices, CAP, -1).astype(jnp.float32), axis=1
    )
    combine = table.astype(jnp.float32) * weights_tok[:, None, :]
    mixed = jnp.einsum("ect,ecd->td", combine, expert_out, precision=lax.Precision.HIGHEST)
    sections = lax.axis_size("section")
    return lax.ppermute(
        mixed.astype(jnp.bfloat16)[None],
        "section",
        [(i, (i + 1) % sections) for i in range(sections)],
    )


def solution(mesh):
    grouped = mesh.shape["ep"] == EXP_WIN * GROUP and mesh.shape["section"] > 2
    return jax.shard_map(
        grouped_body if grouped else general_body,
        mesh=mesh,
        in_specs=(
            P("section", "ep", None),
            P("section", "ep", None),
            P("section", "ep", None),
            P("section", "ep", None),
            P("section", None, "ep"),
            P("section", None, "ep"),
            P("section", "ep", None),
        ),
        out_specs=P("section", "ep", None),
        check_vma=False,
    )
```
